32 devices in a mesh: fsdp: 4 (over z), ctx: 2 (over x), tp: 4 (over y, core).
Axes of the slice: x: 2, y: 2, z: 4, core: 2. Of those that a mesh axis runs over, the one named last changes fastest.
Arguments:
- inputs: bfloat16 [2, 4, 512, 2048], P(None, 'fsdp', 'ctx'), may hold values from -6 to 6
- out_grad: bfloat16 [2, 4, 512, 2048], P(None, 'fsdp', 'ctx'), may hold values from -6 to 6
- segments: int32 [2, 4, 512], P(None, 'fsdp'), may hold values from 0 to 3, never falling along the last dimension, each value on 1 to 384 neighbouring positions
- w_query: bfloat16 [2048, 2048], P('fsdp', 'tp'), may hold values from -0.125 to 0.125
- w_key: bfloat16 [2048, 2048], P('fsdp', 'tp'), may hold values from -0.125 to 0.125
- w_value: bfloat16 [2048, 2048], P('fsdp', 'tp'), may hold values from -0.125 to 0.125
- w_out: bfloat16 [2048, 2048], P('tp', 'fsdp'), may hold values from -0.125 to 0.125
- w_gate: bfloat16 [2048, 8192], P('fsdp', 'tp'), may hold values from -0.125 to 0.125
- w_up: bfloat16 [2048, 8192], P('fsdp', 'tp'), may hold values from -0.125 to 0.125
- w_down: bfloat16 [8192, 2048], P('tp', 'fsdp'), may hold values from -0.0625 to 0.0625
- query_gain: bfloat16 [16, 128], P('tp', 'fsdp'), may hold values from 0.099609375 to 1.8984375
- key_gain: bfloat16 [16, 128], P('tp', 'fsdp'), may hold values from 0.099609375 to 1.8984375
- attn_gain: bfloat16 [2048], P('fsdp'), may hold values from 0.099609375 to 1.8984375
- mlp_gain: bfloat16 [2048], P('fsdp'), may hold values from 0.099609375 to 1.8984375
Outputs:
- output: bfloat16 [2, 4, 512, 2048], P(None, 'fsdp', 'ctx')
- input_grad: float32 [2, 4, 512, 2048], P(None, 'fsdp', 'ctx')
- w_query_grad: float32 [2048, 2048], P('fsdp', 'tp')
- w_key_grad: float32 [2048, 2048], P('fsdp', 'tp')
- w_value_grad: float32 [2048, 2048], P('fsdp', 'tp')
- w_out_grad: float32 [2048, 2048], P('tp', 'fsdp')
- w_gate_grad: float32 [2048, 8192], P('fsdp', 'tp')
- w_up_grad: float32 [2048, 8192], P('fsdp', 'tp')
- w_down_grad: float32 [8192, 2048], P('tp', 'fsdp')
- query_gain_grad: float32 [16, 128], P('tp', 'fsdp')
- key_gain_grad: float32 [16, 128], P('tp', 'fsdp')
- attn_gain_grad: float32 [2048], P('fsdp')
- mlp_gain_grad: float32 [2048], P('fsdp')
The draws below stay inside these ranges and needn't reach their ends.
Inputs may be any that keep to these rules, and one draw needn't show every extreme that they name: `segments`: segment numbers never fall along a sequence; a run of equal numbers is one document, of at most 384 tokens, and one document of each sequence has exactly that many.
All inputs are finite; a program needn't handle non-finite values.
Results may differ from the reference program's by a relative error of at most 0.02.
Values may be sent and summed in bfloat16 or wider, within the bound.
No kernel may reach another device: no remote copies, remote signals or barrier semaphores. Data moves between devices by JAX's collectives and lax.ppermute only.
A program may use at most 192 MiB of HBM per device.

```python
import math
import jax
import jax.numpy as jnp
import numpy as np
from jax import lax

D = 2048
HEADS = 16
HD = 128
FF = 8192
LENGTH = 512
MICRO = 2
SEQS = 4


def shard_levels(rng, dims, shards, low, largest):
    loudness = 1.0
    for dim, blocks in shards:
        draws = jax.random.uniform(jax.random.fold_in(jax.random.fold_in(rng, 6), dim), (blocks,), jnp.float32, low / len(shards), largest / len(shards))
        loudness = loudness * jnp.repeat(jnp.exp(draws), dims[dim] // blocks).reshape((-1,) + (1,) * (len(dims) - 1 - dim))
    return loudness


def profile(count, total, most, slope):
    weights = [(1 << 20) // math.isqrt(rank ** slope) + 1 for rank in range(2, count + 1)]
    surplus, holding = total - most - (count - 1), [1] * (count - 1)
    while surplus > 0:
        free = [i for i in range(count - 1) if holding[i] < most]
        pool, left = sum([weights[i] for i in free]), surplus
        for i in free:
            addition = min(most - holding[i], max(1, left * weights[i] // pool), surplus)
            holding[i] = holding[i] + addition
            surplus = surplus - addition
    return np.array([most] + holding)


def ragged(stream_key, number_of, total, reach, lean):
    if number_of == 2:
        one = jax.random.randint(stream_key, (), max(1, total - reach), min(reach, total - 1) + 1)
        return jnp.stack([one, total - one])
    lengths = jnp.asarray(profile(number_of, total, reach, lean), jnp.int32)
    pairs = (number_of - 1) // 2
    source_of, sink = lengths[1:1 + 2 * pairs:2], lengths[2:2 + 2 * pairs:2]
    room = jnp.minimum(source_of - 1, reach - sink)
    moved = jax.random.randint(jax.random.fold_in(stream_key, 1), (pairs,), 0, 1 << 20) % (room + 1)
    lengths = lengths.at[1:1 + 2 * pairs:2].set(source_of - moved).at[2:2 + 2 * pairs:2].set(sink + moved)
    return lengths[jax.random.permutation(jax.random.fold_in(stream_key, 2), number_of)]


def gaussian(own_key, extent, width, most, pieces=(), kind=jnp.bfloat16):
    drawn = jax.random.normal(own_key, extent, jnp.float32) * width
    if len(pieces) > 0:
        drawn = shard_levels(own_key, extent, pieces, -0.22, 0.18) * drawn
    return jnp.clip(drawn, min=-most, max=most).astype(kind)


def setup_inputs(seed: int = 0) -> dict:
    keys = jax.random.split(jax.random.key(seed), 15)
    inputs = gaussian(keys[0], (MICRO, SEQS, LENGTH, D), 1.0, 6.0, ((1, 4), (2, 2)))
    out_grad = gaussian(keys[1], (MICRO, SEQS, LENGTH, D), 1.0, 6.0, ((1, 4), (2, 2)))
    segments = jax.vmap(lambda own: jnp.searchsorted(jnp.cumsum(ragged(own, max(2, LENGTH // 128), LENGTH, LENGTH * 3 // 4, 1)), jnp.arange(LENGTH), side="right"))(jax.random.split(keys[2], MICRO * SEQS)).reshape((MICRO, SEQS, LENGTH)).astype(jnp.int32)
    w_query = gaussian(keys[3], (D, D), D ** -0.5, 0.125, ((0, 4), (1, 4)))
    w_key = gaussian(keys[4], (D, D), D ** -0.5, 0.125, ((0, 4), (1, 4)))
    w_value = gaussian(keys[5], (D, D), D ** -0.5, 0.125, ((0, 4), (1, 4)))
    w_out = gaussian(keys[6], (D, D), D ** -0.5, 0.125, ((0, 4), (1, 4)))
    w_gate = gaussian(keys[7], (D, FF), D ** -0.5, 0.125, ((0, 4), (1, 4)))
    w_up = gaussian(keys[8], (D, FF), D ** -0.5, 0.125, ((0, 4), (1, 4)))
    w_down = gaussian(keys[9], (FF, D), FF ** -0.5, 0.0625, ((0, 4), (1, 4)))
    query_gain = jnp.clip(1.0 + 0.18 * jax.random.normal(keys[10], (HEADS, HD), jnp.float32), 0.099609375, 1.8984375).astype(jnp.bfloat16)
    key_gain = jnp.clip(1.0 + 0.18 * jax.random.normal(keys[11], (HEADS, HD), jnp.float32), 0.099609375, 1.8984375).astype(jnp.bfloat16)
    attn_gain = jnp.clip(1.0 + 0.18 * jax.random.normal(keys[12], (D,), jnp.float32), 0.099609375, 1.8984375).astype(jnp.bfloat16)
    mlp_gain = jnp.clip(1.0 + 0.18 * jax.random.normal(keys[13], (D,), jnp.float32), 0.099609375, 1.8984375).astype(jnp.bfloat16)
    return dict(inputs=inputs, out_grad=out_grad, segments=segments, w_query=w_query, w_key=w_key, w_value=w_value, w_out=w_out, w_gate=w_gate, w_up=w_up, w_down=w_down, query_gain=query_gain, key_gain=key_gain, attn_gain=attn_gain, mlp_gain=mlp_gain)


@jax.custom_vjp
def low(v):
    return lax.optimization_barrier(v.astype(jnp.bfloat16)).astype(jnp.float32)

@jax.custom_vjp
def low_back(v):
    return v

def low_keep(v):
    return (low(v), None)

def low_pass(kept, grad):
    return (grad,)

def back_keep(v):
    return (v, None)

def back_low(kept, grad):
    return (low(grad),)
low.defvjp(low_keep, low_pass)
low_back.defvjp(back_keep, back_low)
EPSILON = 1e-06
ROTARY_BASE = 500000.0

def product(left_side, right_side):
    return jnp.dot(left_side, right_side, precision=lax.Precision.HIGHEST, preferred_element_type=jnp.float32)

def rms_norm(values, gain_row):
    return values * lax.rsqrt(lax.optimization_barrier(jnp.mean(values * values, axis=-1, keepdims=True)) + EPSILON) * gain_row

def doc_positions(segment_row):
    earlier = (segment_row[None, :] < segment_row[:, None]).astype(jnp.int32)
    return jnp.arange(segment_row.shape[0], dtype=jnp.int32) - lax.optimization_barrier(jnp.sum(earlier, axis=1)).astype(jnp.int32)

def rotary_tables(positions):
    half_size = HD // 2
    frequency = ROTARY_BASE ** (-(jnp.arange(half_size, dtype=jnp.float32) * 2.0 / HD))
    angle_table = positions.astype(jnp.float32)[:, None] * frequency[None, :]
    return (jnp.cos(angle_table)[:, None, :], jnp.sin(angle_table)[:, None, :])

def rotate(values, cosine, sine_table):
    half_size = values.shape[-1] // 2
    first_half = values[..., :half_size]
    second_half = values[..., half_size:]
    return jnp.concatenate([first_half * cosine - second_half * sine_table, second_half * cosine + first_half * sine_table], axis=-1)

def layer_forward(tokens_in, segment_row, weights):
    w_query, w_key, w_value, w_out, w_gate, w_up, w_down, query_gain, key_gain, attn_gain, mlp_gain = weights
    length = tokens_in.shape[0]
    cosine, sine_table = rotary_tables(doc_positions(segment_row))
    query_raw = low_back(product(tokens_in, w_query))
    key_raw = low_back(product(tokens_in, w_key))
    value_low = low_back(low(product(tokens_in, w_value))).reshape(length, HEADS, HD)
    query_norm = rms_norm(query_raw, query_gain.reshape(-1)).reshape(length, HEADS, HD)
    key_norm = rms_norm(key_raw, key_gain.reshape(-1)).reshape(length, HEADS, HD)
    query_rot = low_back(low(rotate(query_norm, cosine, sine_table)))
    key_rot = low_back(low(rotate(key_norm, cosine, sine_table)))
    scores = low_back(jnp.einsum('qhd,khd->hqk', query_rot, key_rot, precision=lax.Precision.HIGHEST) / math.sqrt(HD))
    places = jnp.arange(length)
    allowed = (segment_row[:, None] == segment_row[None, :]) & (places[None, :] <= places[:, None])
    scores = jnp.where(allowed[None], scores, -1e+30)
    attn_probs = low(jax.nn.softmax(scores, axis=-1))
    attended = low_back(low(jnp.einsum('hqk,khd->qhd', attn_probs, value_low, precision=lax.Precision.HIGHEST)))
    branch = low_back(product(attended.reshape(length, D), w_out))
    hidden_in = tokens_in + rms_norm(branch, attn_gain)
    hidden_low = low(hidden_in)
    gate_value = low_back(product(hidden_low, w_gate))
    up_value = low_back(product(hidden_low, w_up))
    activated = low(jax.nn.silu(gate_value) * up_value)
    down_value = low_back(product(activated, w_down))
    return hidden_in + rms_norm(down_value, mlp_gain)

def reference(inputs, out_grad, segments, w_query, w_key, w_value, w_out, w_gate, w_up, w_down, query_gain, key_gain, attn_gain, mlp_gain):
    weights = tuple((argument.astype(jnp.float32) for argument in (w_query, w_key, w_value, w_out, w_gate, w_up, w_down, query_gain, key_gain, attn_gain, mlp_gain)))
    flat_inputs = inputs.astype(jnp.float32).reshape(MICRO * SEQS, LENGTH, D)
    flat_cotangent = out_grad.astype(jnp.float32).reshape(MICRO * SEQS, LENGTH, D)
    flat_segments = segments.reshape(MICRO * SEQS, LENGTH)

    def one_sequence(totals, sequence):
        tokens_in, cotangent, segment_row = sequence

        def forward(tokens_arg, weights_arg):
            return layer_forward(tokens_arg, segment_row, weights_arg)
        result, pullback = jax.vjp(forward, tokens_in, weights)
        input_part, weight_grads = pullback(cotangent)
        totals = jax.tree.map(lambda running, addend: running + addend, totals, weight_grads)
        return (totals, (result.astype(jnp.bfloat16), input_part))
    zero_grads = tuple((jnp.zeros_like(argument) for argument in weights))
    totals, (outputs, input_grads) = lax.scan(one_sequence, zero_grads, (flat_inputs, flat_cotangent, flat_segments))
    out_shape = (MICRO, SEQS, LENGTH, D)
    return (outputs.reshape(out_shape), input_grads.reshape(out_shape), totals[0], totals[1], totals[2], totals[3], totals[4], totals[5], totals[6], totals[7], totals[8], totals[9], totals[10])
```

```python
import math

import jax
import jax.numpy as jnp
from jax import lax
from jax.sharding import PartitionSpec as P

D = 2048
HD = 128
EPSILON = 1e-06
ROTARY_BASE = 500000.0
MASKED = -1e30
GAIN_ROWS = 16
LOW = jnp.bfloat16
WIDE = jnp.float32


def product(left_side, right_side):
    return jnp.dot(left_side, right_side, preferred_element_type=WIDE)


def product_back(left_side, right_side):
    return lax.dot_general(
        left_side, right_side, (((1,), (1,)), ((), ())), preferred_element_type=WIDE
    )


def product_left(left_side, right_side):
    return lax.dot_general(
        left_side, right_side, (((0,), (0,)), ((), ())), preferred_element_type=WIDE
    )


def doc_positions(segment_row):
    earlier = (segment_row[None, :] < segment_row[:, None]).astype(jnp.int32)
    return jnp.arange(segment_row.shape[0], dtype=jnp.int32) - jnp.sum(earlier, axis=1)


def rotary_tables(positions):
    half_size = HD // 2
    frequency = ROTARY_BASE ** (-(jnp.arange(half_size, dtype=WIDE) * 2.0 / HD))
    angle_table = positions.astype(WIDE)[:, None] * frequency[None, :]
    return (jnp.cos(angle_table)[:, None, :], jnp.sin(angle_table)[:, None, :])


def rotate(values, cosine, sine_table):
    half_size = values.shape[-1] // 2
    first_half = values[..., :half_size]
    second_half = values[..., half_size:]
    return jnp.concatenate(
        [
            first_half * cosine - second_half * sine_table,
            second_half * cosine + first_half * sine_table,
        ],
        axis=-1,
    )


def attention_mask(segment_row):
    places = jnp.arange(segment_row.shape[0])
    return (segment_row[:, None] == segment_row[None, :]) & (places[None, :] <= places[:, None])


def head_scores(query_heads, key_heads, allowed):
    raw_scores = jnp.einsum(
        "qhd,khd->hqk", query_heads, key_heads, preferred_element_type=WIDE
    ) * (1.0 / math.sqrt(HD))
    return jnp.where(allowed[None], raw_scores, MASKED)


def flip(value, axis, bit, size):
    return lax.ppermute(value, axis, [(place, place ^ bit) for place in range(size)])


def after(value, *earlier):
    return lax.optimization_barrier((value,) + earlier)[0]


def solution(mesh):
    fsdp = mesh.shape["fsdp"]
    ctx = mesh.shape["ctx"]
    tp = mesh.shape["tp"]

    def shift(value, step):
        return lax.ppermute(
            value, "fsdp", [(place, (place - step) % fsdp) for place in range(fsdp)]
        )

    def swap(value):
        return flip(value, "ctx", 1, ctx)

    def tp_gather(block):
        second = flip(block, "tp", 2, tp)
        pair = jnp.concatenate([block, second], axis=0)
        return jnp.concatenate([pair, flip(pair, "tp", 1, tp)], axis=0)

    def tp_scatter(make, rows):
        half = rows[0].shape[0] // 2
        sent = make(*(part[half:] for part in rows)).astype(LOW)
        got = flip(sent, "tp", 1, tp)
        kept = make(*(part[:half] for part in rows)) + got.astype(WIDE)
        again = flip(kept[half // 2 :].astype(LOW), "tp", 2, tp)
        return kept[: half // 2] + again.astype(WIDE)

    def local(
        inputs,
        out_grad,
        segments,
        w_query,
        w_key,
        w_value,
        w_out,
        w_gate,
        w_up,
        w_down,
        query_gain,
        key_gain,
        attn_gain,
        mlp_gain,
    ):
        f = lax.axis_index("fsdp")
        c = lax.axis_index("ctx")
        t = lax.axis_index("tp")
        half_len = inputs.shape[2]
        length = half_len * ctx
        part_len = length // tp
        block = D // fsdp
        half_block = block // 2
        heads_here = query_gain.shape[0]
        width = heads_here * HD
        hidden_here = w_gate.shape[1] // fsdp
        scale_factor = 1.0 / math.sqrt(HD)
        first = c == 0

        def pair(own, other, axis):
            return jnp.where(
                first,
                jnp.concatenate([own, other], axis=axis),
                jnp.concatenate([other, own], axis=axis),
            )

        def near_rows(value):
            return jnp.concatenate(
                [
                    lax.dynamic_slice_in_dim(value, (t ^ bit) * part_len, part_len, 0)
                    for bit in (0, 2, 1, 3)
                ],
                axis=0,
            )

        def plain_rows(value, size):
            parts = []
            for place in range(tp):
                far = t ^ place
                spot = (far & 1) * 2 + (far >> 1)
                parts.append(lax.dynamic_slice_in_dim(value, spot * size, size, 0))
            return jnp.concatenate(parts, axis=0)

        def place(r):
            return lax.rem(f + (r % fsdp), fsdp)

        gain_pack = jnp.concatenate(
            [query_gain.reshape(-1), key_gain.reshape(-1), attn_gain, mlp_gain]
        )
        gain_rows = jnp.pad(gain_pack, (0, GAIN_ROWS * 2 * width - gain_pack.size)).reshape(
            GAIN_ROWS, 2 * width
        )

        def half_of(shard, side):
            return lax.dynamic_slice_in_dim(shard, side * half_block, half_block, 0)

        def ring(own, more):
            moving = half_of(own, c)
            if more is not None:
                moving = jnp.concatenate([moving, more], axis=0)
            whole = lax.dynamic_update_slice(
                jnp.zeros((D, own.shape[1]), LOW), own, (f * block, 0)
            )
            moved = [moving]
            for r in range(1, fsdp):
                moved.append(shift(moved[-1], 1))
                got = moved[-1][:half_block]
                begin = place(r) * block
                whole = lax.dynamic_update_slice(whole, got, (begin + c * half_block, 0))
                whole = lax.dynamic_update_slice(
                    whole, swap(got), (begin + (1 - c) * half_block, 0)
                )
            return whole, moved

        qk_full, qk_moved = ring(jnp.concatenate([w_query, w_key], axis=1), gain_rows)
        vo_full, vo_moved = ring(jnp.concatenate([w_value, w_out.T], axis=1), None)
        value_full, out_full = vo_full[:, :width], vo_full[:, width:]

        gain_near = jnp.stack([part[half_block:].reshape(-1) for part in qk_moved]).astype(WIDE)
        gain_all = lax.dynamic_slice_in_dim(
            jnp.concatenate([gain_near, gain_near], axis=0), lax.rem(fsdp - f, fsdp), fsdp, 0
        )
        qk_size = query_gain.size
        query_gain_row = (
            gain_all[:, :qk_size].reshape(fsdp, heads_here, -1).transpose(1, 0, 2).reshape(-1)
        )
        key_gain_row = (
            gain_all[:, qk_size : 2 * qk_size]
            .reshape(fsdp, heads_here, -1)
            .transpose(1, 0, 2)
            .reshape(-1)
        )
        attn_gains = gain_all[:, 2 * qk_size : 2 * qk_size + block].reshape(1, -1)
        mlp_gains = gain_all[:, 2 * qk_size + block : 2 * (qk_size + block)].reshape(1, -1)

        sub_len = half_len // tp
        tokens_kept = lax.dynamic_index_in_dim(inputs[:, 0], c, 0, keepdims=False)
        tokens_sent = lax.dynamic_slice(
            inputs, (1 - c, 0, t * sub_len, 0), (1, 1, sub_len, D)
        )[0, 0]
        tokens_got = plain_rows(tp_gather(swap(tokens_sent)), sub_len)
        tokens = pair(tokens_kept, tokens_got, 0)
        segment_row = lax.dynamic_index_in_dim(segments[:, 0], c, 0, keepdims=False)

        half_hidden = hidden_here // 2

        def fetch_rows(shard):
            mine = half_of(shard, c).reshape(half_block, fsdp, hidden_here).transpose(1, 0, 2)
            mine = lax.all_to_all(mine, "fsdp", 0, 0, tiled=True)
            return pair(mine[:, None], swap(mine)[:, None], 1).reshape(D, hidden_here)

        def fetch_columns(shard):
            mine = shard.reshape(fsdp, 2, half_hidden, block)
            mine = lax.dynamic_index_in_dim(mine, c, 1, keepdims=False)
            mine = lax.all_to_all(mine, "fsdp", 0, 0, tiled=True)
            whole = pair(mine[:, None], swap(mine)[:, None], 1)
            return whole.reshape(fsdp, hidden_here, block).transpose(1, 0, 2).reshape(-1, D)

        gate_late, up_late, down_late = lax.optimization_barrier(
            (w_gate, w_up, w_down, qk_moved[-1])
        )[:3]
        wide_full = jnp.concatenate([fetch_rows(gate_late), fetch_rows(up_late)], axis=1)
        down_full = fetch_columns(down_late)

        allowed = attention_mask(segment_row)
        cosine, sine_table = rotary_tables(doc_positions(segment_row))
        raw = product(tokens, qk_full)
        query_raw = raw[:, :width]
        key_raw = raw[:, width:]
        value_heads = product(tokens, value_full).astype(LOW).reshape(length, heads_here, HD)
        squares = lax.psum(
            jnp.stack([jnp.sum(query_raw * query_raw, axis=1), jnp.sum(key_raw * key_raw, axis=1)]),
            "tp",
        )
        query_scale = lax.rsqrt(squares[0] / D + EPSILON)[:, None]
        key_scale = lax.rsqrt(squares[1] / D + EPSILON)[:, None]
        query_heads = rotate(
            (query_raw * query_scale * query_gain_row).reshape(length, heads_here, HD),
            cosine,
            sine_table,
        ).astype(LOW)
        key_heads = rotate(
            (key_raw * key_scale * key_gain_row).reshape(length, heads_here, HD),
            cosine,
            sine_table,
        ).astype(LOW)
        scores = head_scores(query_heads, key_heads, allowed)
        top_score = jnp.max(scores, axis=-1, keepdims=True)
        log_total = top_score + jnp.log(
            jnp.sum(jnp.exp(scores - top_score), axis=-1, keepdims=True)
        )
        probs_low = jnp.exp(scores - log_total).astype(LOW)
        attended = (
            jnp.einsum("hqk,khd->qhd", probs_low, value_heads, preferred_element_type=WIDE)
            .astype(LOW)
            .reshape(length, width)
        )
        attended_near = near_rows(attended)
        branch = tp_scatter(lambda rows: product_back(rows, out_full), (attended_near,))

        tokens_part = lax.dynamic_slice_in_dim(tokens, t * part_len, part_len, 0).astype(WIDE)
        branch_scale = lax.rsqrt(jnp.mean(branch * branch, axis=-1, keepdims=True) + EPSILON)
        hidden = tokens_part + branch * branch_scale * attn_gains
        hidden_low = hidden.astype(LOW)

        group_size = min(fsdp, 4)

        def all_chunks(part):
            moved = [part]
            for _ in range(1, fsdp):
                moved.append(shift(moved[-1], 1))
            groups = []
            for g in range(0, fsdp, group_size):
                group = jnp.zeros((group_size * length, D), LOW)
                for r in range(group_size):
                    second = flip(moved[g + r], "tp", 2, tp)
                    both = jnp.concatenate([moved[g + r], second], axis=0)
                    third = flip(both, "tp", 1, tp)
                    group = lax.dynamic_update_slice(group, both, (r * length, 0))
                    group = lax.dynamic_update_slice(
                        group, third, (r * length + length // 2, 0)
                    )
                groups.append(group)
            return groups, [
                group[r * length : (r + 1) * length] for group in groups for r in range(group_size)
            ]

        def all_tokens(left_groups, right_groups):
            total = product_left(left_groups[0], right_groups[0])
            for left_side, right_side in zip(left_groups[1:], right_groups[1:]):
                total = total + product_left(left_side, right_side)
            return total.astype(LOW)

        def grouped(chunks):
            return [
                jnp.concatenate(chunks[g : g + group_size], axis=0)
                for g in range(0, fsdp, group_size)
            ]

        def to_owner(parts):
            total = parts[0]
            for r in range(1, fsdp):
                total = total + shift(parts[r].astype(LOW), -r).astype(WIDE)
            return total

        hidden_all, hidden_chunks = all_chunks(hidden_low)
        wide_chunks, active_chunks, down_parts = [], [], []
        for chunk in hidden_chunks:
            wide = product(chunk, wide_full)
            gate_value, up_value = wide[:, :hidden_here], wide[:, hidden_here:]
            active = (gate_value * jax.nn.sigmoid(gate_value) * up_value).astype(LOW)
            down_parts.append(tp_scatter(lambda rows: product(rows, down_full), (active,)))
            wide_chunks.append(wide)
            active_chunks.append(active)
        down = to_owner(down_parts)

        down_scale = lax.rsqrt(jnp.mean(down * down, axis=-1, keepdims=True) + EPSILON)
        output_part = (hidden + down * down_scale * mlp_gains).astype(LOW)

        inner = lax.rem(t, tp // 2) * part_len
        grad_kept = lax.dynamic_slice(
            out_grad, (c, 0, inner, 0), (1, 1, part_len, D)
        )[0, 0]
        grad_sent = lax.dynamic_slice(
            out_grad, (1 - c, 0, inner, 0), (1, 1, part_len, D)
        )[0, 0]
        mine_here = t // (tp // 2) == c
        cotangent = jnp.where(
            mine_here, grad_kept, swap(after(grad_sent, qk_moved[-1]))
        ).astype(WIDE)

        scaled = cotangent * mlp_gains
        down_mean = jnp.mean(scaled * down, axis=-1, keepdims=True)
        down_low = (down_scale * (scaled - down * (down_scale * down_scale * down_mean))).astype(
            LOW
        )
        mlp_gain_grad = jnp.sum(cotangent * down * down_scale, axis=0)

        grad_all, grad_chunks = all_chunks(down_low)
        wide_lows, hidden_parts = [], []
        for chunk, wide in zip(grad_chunks, wide_chunks):
            gate_value, up_value = wide[:, :hidden_here], wide[:, hidden_here:]
            act_grad = product_back(chunk, down_full)
            sig = jax.nn.sigmoid(gate_value)
            gate_low = (act_grad * up_value * sig * (1.0 + gate_value * (1.0 - sig))).astype(LOW)
            up_low = (act_grad * gate_value * sig).astype(LOW)
            wide_low = jnp.concatenate([gate_low, up_low], axis=1)
            hidden_parts.append(
                tp_scatter(lambda rows: product_back(rows, wide_full), (wide_low,))
            )
            wide_lows.append(wide_low)
        hidden_grad = cotangent + to_owner(hidden_parts)

        def half_sum(split, earlier):
            sent = lax.dynamic_index_in_dim(split, 1 - c, 1, keepdims=False)
            kept = lax.dynamic_index_in_dim(split, c, 1, keepdims=False)
            got = swap(sent if earlier is None else after(sent, earlier))
            return (kept.astype(WIDE) + got.astype(WIDE)).astype(LOW)

        down_grads = all_tokens(grouped(active_chunks), grad_all)
        down_split = down_grads.reshape(2, half_hidden, fsdp, block).transpose(2, 0, 1, 3)
        down_sum = half_sum(down_split, None)
        wide_grads = all_tokens(hidden_all, grouped(wide_lows))
        wide_split = wide_grads.reshape(fsdp, 2, half_block, 2 * hidden_here)
        gate_sum = half_sum(wide_split[..., :hidden_here], down_sum)
        up_sum = half_sum(wide_split[..., hidden_here:], gate_sum)

        def both_sides(summed):
            mine = lax.all_to_all(after(summed, hidden_grad), "fsdp", 0, 0, tiled=True)
            return lax.all_gather(mine, "ctx", axis=0)

        grad_down = both_sides(down_sum).transpose(1, 0, 2, 3).reshape(-1, block).astype(WIDE)
        grad_gate = both_sides(gate_sum).transpose(0, 2, 1, 3).reshape(block, -1).astype(WIDE)
        grad_up = both_sides(up_sum).transpose(0, 2, 1, 3).reshape(block, -1).astype(WIDE)

        lifted = hidden_grad * attn_gains
        branch_mean = jnp.mean(lifted * branch, axis=-1, keepdims=True)
        branch_low = (
            branch_scale * (lifted - branch * (branch_scale * branch_scale * branch_mean))
        ).astype(LOW)
        attn_gain_grad = jnp.sum(hidden_grad * branch * branch_scale, axis=0)
        branch_near = tp_gather(branch_low)
        heads_grad = plain_rows(
            product(branch_near, out_full).astype(LOW), part_len
        ).reshape(length, heads_here, HD)
        attn_probs = jnp.exp(head_scores(query_heads, key_heads, allowed) - log_total)
        value_grad = (
            jnp.einsum(
                "hqk,qhd->khd", attn_probs.astype(LOW), heads_grad, preferred_element_type=WIDE
            )
            .astype(LOW)
            .reshape(length, width)
        )
        probs_grad = jnp.einsum(
            "qhd,khd->hqk", heads_grad, value_heads, preferred_element_type=WIDE
        )
        score_grad = (
            attn_probs * (probs_grad - jnp.sum(attn_probs * probs_grad, axis=-1, keepdims=True))
        ).astype(LOW)
        query_grad = (
            jnp.einsum("hqk,khd->qhd", score_grad, key_heads, preferred_element_type=WIDE)
            * scale_factor
        )
        key_grad = (
            jnp.einsum("hqk,qhd->khd", score_grad, query_heads, preferred_element_type=WIDE)
            * scale_factor
        )
        query_norm_grad = rotate(query_grad, cosine, -sine_table).reshape(length, width)
        key_norm_grad = rotate(key_grad, cosine, -sine_table).reshape(length, width)
        query_term = query_norm_grad * query_gain_row
        key_term = key_norm_grad * key_gain_row
        dots = lax.psum(
            jnp.stack(
                [jnp.sum(query_term * query_raw, axis=1), jnp.sum(key_term * key_raw, axis=1)]
            ),
            "tp",
        )
        query_cube = query_scale * query_scale * query_scale
        key_cube = key_scale * key_scale * key_scale
        query_raw_grad = (
            query_scale * query_term - query_raw * (query_cube * dots[0][:, None] / D)
        ).astype(LOW)
        key_raw_grad = (
            key_scale * key_term - key_raw * (key_cube * dots[1][:, None] / D)
        ).astype(LOW)
        query_gain_grad = jnp.sum(query_norm_grad * query_raw * query_scale, axis=0)
        key_gain_grad = jnp.sum(key_norm_grad * key_raw * key_scale, axis=0)
        qk_grad = jnp.concatenate([query_raw_grad, key_raw_grad], axis=1)

        def gathered(partial, dim):
            mine = lax.psum_scatter(partial, "fsdp", scatter_dimension=dim, tiled=True)
            return lax.psum(mine, "ctx").astype(WIDE)

        grad_out = gathered(product_left(attended_near, branch_near).astype(LOW), 1)
        grad_value = gathered(product_left(tokens, value_grad).astype(LOW), 0)

        def row_shard(grads):
            summed = half_sum(grads.astype(LOW).reshape(fsdp, 2, half_block, width), None)
            parts = lax.all_to_all(summed, "fsdp", 0, 0, tiled=True)
            mine = jnp.sum(parts.astype(WIDE), axis=0).astype(LOW)
            mine = lax.optimization_barrier(mine)
            return pair(mine, swap(mine), 0).astype(WIDE)

        grad_query = row_shard(product_left(tokens, query_raw_grad))
        grad_key = row_shard(product_left(tokens, key_raw_grad))

        input_part = hidden_grad + tp_scatter(
            lambda rows, more: product_back(rows, qk_full) + product_back(more, value_full),
            (near_rows(qk_grad), near_rows(value_grad)),
        )

        def spread(part):
            part = lax.optimization_barrier(part.astype(LOW))
            pairs = []
            for low_place in range(tp // 2):
                here, there = tp // 2 + low_place, tp + low_place
                pairs += [(here, there), (there, here)]
            got = lax.ppermute(part, ("ctx", "tp"), pairs)
            near = jnp.where(mine_here, part, got)
            far = flip(near, "tp", 2, tp)
            mine = jnp.where(mine_here, near, far)
            other = jnp.where(mine_here, far, near)
            both = jnp.where(
                first, jnp.stack([mine, other]), jnp.stack([other, mine])
            )
            beside = flip(both, "tp", 1, tp)
            return jnp.where(
                t % 2 == 0,
                jnp.concatenate([both, beside], axis=1),
                jnp.concatenate([beside, both], axis=1),
            )[:, None]

        layer_out = spread(after(output_part, hidden_grad))
        layer_in_grad = spread(input_part).astype(WIDE)

        rows_grad = jnp.stack([attn_gain_grad, mlp_gain_grad])
        for bit in (1, 2):
            rows_grad = rows_grad + flip(rows_grad, "tp", bit, tp)
        packed = jnp.concatenate(
            [
                rows_grad.reshape(2, fsdp, block).transpose(1, 0, 2).reshape(fsdp, 2 * block),
                jnp.stack([query_gain_grad, key_gain_grad])
                .reshape(2 * heads_here, fsdp, HD // fsdp)
                .transpose(1, 0, 2)
                .reshape(fsdp, -1),
            ],
            axis=1,
        )
        packed = packed + swap(packed)
        own_gains = lax.dynamic_index_in_dim(packed, f, 0, keepdims=False)
        for r in range(1, fsdp):
            own_gains = own_gains + shift(
                lax.dynamic_index_in_dim(packed, place(r), 0, keepdims=False), -r
            )
        sum_heads = own_gains[2 * block :].reshape(2, heads_here, HD // fsdp)
        return (
            layer_out,
            layer_in_grad,
            grad_query,
            grad_key,
            grad_value,
            grad_out,
            grad_gate,
            grad_up,
            grad_down,
            sum_heads[0],
            sum_heads[1],
            own_gains[:block],
            own_gains[block : 2 * block],
        )

    rows = P("fsdp", "tp")
    columns = P("tp", "fsdp")
    whole_tokens = P(None, "fsdp", "ctx", None)
    return jax.shard_map(
        local,
        mesh=mesh,
        in_specs=(
            whole_tokens,
            whole_tokens,
            P(None, "fsdp", None),
            rows,
            rows,
            rows,
            columns,
            rows,
            rows,
            columns,
            columns,
            columns,
            P("fsdp"),
            P("fsdp"),
        ),
        out_specs=(
            whole_tokens,
            whole_tokens,
            rows,
            rows,
            rows,
            columns,
            rows,
            rows,
            columns,
            columns,
            columns,
            P("fsdp"),
            P("fsdp"),
        ),
        check_vma=False,
    )
```

```python
import math

import jax
import jax.numpy as jnp
from jax import lax
from jax.experimental import pallas as pl
from jax.experimental.layout import Layout, with_layout_constraint
from jax.experimental.pallas import tpu as pltpu
from jax.sharding import PartitionSpec as P

D = 2048
HD = 128
EPSILON = 1e-06
ROTARY_BASE = 500000.0
MASKED = -1e30
LOW = jnp.bfloat16
WIDE = jnp.float32


def product(left_side, right_side):
    return jnp.dot(left_side, right_side, preferred_element_type=WIDE)


def product_back(left_side, right_side):
    return lax.dot_general(
        left_side, right_side, (((1,), (1,)), ((), ())), preferred_element_type=WIDE
    )


def product_left(left_side, right_side):
    return lax.dot_general(
        left_side, right_side, (((0,), (0,)), ((), ())), preferred_element_type=WIDE
    )


def doc_positions(segment_row):
    earlier = (segment_row[None, :] < segment_row[:, None]).astype(jnp.int32)
    return jnp.arange(segment_row.shape[0], dtype=jnp.int32) - jnp.sum(earlier, axis=1)


def rotary_tables(positions):
    half_size = HD // 2
    frequency = ROTARY_BASE ** (-(jnp.arange(half_size, dtype=WIDE) * 2.0 / HD))
    angle_table = positions.astype(WIDE)[:, None] * frequency[None, :]
    return (jnp.cos(angle_table)[:, None, :], jnp.sin(angle_table)[:, None, :])


def rotate(values, cosine, sine_table):
    half_size = values.shape[-1] // 2
    first_half = values[..., :half_size]
    second_half = values[..., half_size:]
    return jnp.concatenate(
        [
            first_half * cosine - second_half * sine_table,
            second_half * cosine + first_half * sine_table,
        ],
        axis=-1,
    )


def attention_mask(segment_row):
    places = jnp.arange(segment_row.shape[0])
    return (segment_row[:, None] == segment_row[None, :]) & (places[None, :] <= places[:, None])


def head_scores(query_heads, key_heads, allowed):
    raw_scores = jnp.einsum(
        "qhd,khd->hqk", query_heads, key_heads, preferred_element_type=WIDE
    ) * (1.0 / math.sqrt(HD))
    return jnp.where(allowed[None], raw_scores, MASKED)


def grad_blocks(lefts, rights, fsdp, split_left):
    rows, columns = lefts[0].shape[1], rights[0].shape[1]
    if split_left:
        rows = rows // fsdp
    else:
        columns = columns // fsdp
    half = rows // 2

    def kernel(*refs):
        left_refs, right_refs = refs[: len(lefts)], refs[len(lefts) : -1]
        out_ref = refs[-1]
        pieces = max(len(lefts), len(rights))

        def part(group, number):
            per = pieces // len(group)
            ref = group[number // per]
            size = ref.shape[0] // per
            start = (number % per) * size
            return ref[start : start + size, :]

        total = 0.0
        for number in range(pieces):
            total = total + lax.dot_general(
                part(left_refs, number),
                part(right_refs, number),
                (((0,), (0,)), ((), ())),
                preferred_element_type=WIDE,
            )
        out_ref[0, 0] = total[:half].astype(LOW)
        out_ref[1, 0] = total[half:].astype(LOW)

    def moving(size, width):
        return pl.BlockSpec((size, width), lambda g: (0, g))

    def fixed(size, width):
        return pl.BlockSpec((size, width), lambda g: (0, 0))

    left_spec, right_spec = (moving, fixed) if split_left else (fixed, moving)
    return pl.pallas_call(
        kernel,
        grid=(fsdp,),
        in_specs=[left_spec(left.shape[0], rows) for left in lefts]
        + [right_spec(right.shape[0], columns) for right in rights],
        out_specs=pl.BlockSpec((2, 1, half, columns), lambda g: (0, g, 0, 0)),
        out_shape=jax.ShapeDtypeStruct((2, fsdp, half, columns), LOW),
        compiler_params=pltpu.CompilerParams(vmem_limit_bytes=50 * 1024 * 1024),
        cost_estimate=pl.CostEstimate(flops=1, bytes_accessed=1, transcendentals=0),
    )(*lefts, *rights)


def pack_sends(side, w_gate, w_up, w_down, fsdp):
    rows, hidden = w_gate.shape[0] // 2, w_gate.shape[1] // fsdp
    down_rows, columns = hidden // 2, w_down.shape[1]

    def kernel(side_ref, gate_ref, up_ref, down_ref, gate_out, up_out, down_out):
        gate_out[0] = gate_ref[...]
        up_out[0] = up_ref[...]
        down_out[0] = down_ref[...]

    wide_in = pl.BlockSpec((rows, hidden), lambda g, chosen: (chosen[0], g))
    wide_out = pl.BlockSpec((1, rows, hidden), lambda g, chosen: (g, 0, 0))
    return pl.pallas_call(
        kernel,
        grid_spec=pltpu.PrefetchScalarGridSpec(
            num_scalar_prefetch=1,
            grid=(fsdp,),
            in_specs=[
                wide_in,
                wide_in,
                pl.BlockSpec((down_rows, columns), lambda g, chosen: (2 * g + chosen[0], 0)),
            ],
            out_specs=[
                wide_out,
                wide_out,
                pl.BlockSpec((1, down_rows, columns), lambda g, chosen: (g, 0, 0)),
            ],
        ),
        out_shape=[
            jax.ShapeDtypeStruct((fsdp, rows, hidden), w_gate.dtype),
            jax.ShapeDtypeStruct((fsdp, rows, hidden), w_gate.dtype),
            jax.ShapeDtypeStruct((fsdp, down_rows, columns), w_gate.dtype),
        ],
    )(side, w_gate, w_up, w_down)


def place_wide(side, gate_own, gate_other, up_own, up_other):
    fsdp, rows, hidden = gate_own.shape

    def kernel(side_ref, gate_a, gate_b, up_a, up_b, out_ref):
        for value in range(2):

            @pl.when(side_ref[0] == value)
            def _():
                mine = slice(value * rows, (value + 1) * rows)
                others = slice((1 - value) * rows, (2 - value) * rows)
                out_ref[mine, :hidden] = gate_a[0]
                out_ref[others, :hidden] = gate_b[0]
                out_ref[mine, hidden:] = up_a[0]
                out_ref[others, hidden:] = up_b[0]

    piece = pl.BlockSpec((1, rows, hidden), lambda g: (g, 0, 0))
    return pl.pallas_call(
        kernel,
        grid=(fsdp,),
        in_specs=[pl.BlockSpec(memory_space=pltpu.SMEM)] + [piece] * 4,
        out_specs=pl.BlockSpec((2 * rows, 2 * hidden), lambda g: (g, 0)),
        out_shape=jax.ShapeDtypeStruct((fsdp * 2 * rows, 2 * hidden), gate_own.dtype),
    )(side, gate_own, gate_other, up_own, up_other)


def place_down(side, own, other):
    fsdp, rows, columns = own.shape

    def kernel(side_ref, own_ref, other_ref, out_ref):
        for value in range(2):

            @pl.when(side_ref[0] == value)
            def _():
                out_ref[value * rows : (value + 1) * rows, :] = own_ref[0]
                out_ref[(1 - value) * rows : (2 - value) * rows, :] = other_ref[0]

    piece = pl.BlockSpec((1, rows, columns), lambda g: (g, 0, 0))
    return pl.pallas_call(
        kernel,
        grid=(fsdp,),
        in_specs=[pl.BlockSpec(memory_space=pltpu.SMEM), piece, piece],
        out_specs=pl.BlockSpec((2 * rows, columns), lambda g: (0, g)),
        out_shape=jax.ShapeDtypeStruct((2 * rows, fsdp * columns), own.dtype),
    )(side, own, other)


def widen_rows(side, own, other, parts):
    fsdp, rows, columns = own.shape
    hidden = columns // parts

    def kernel(side_ref, own_ref, other_ref, *out_refs):
        for value in range(2):

            @pl.when(side_ref[0] == value)
            def _():
                for number, out_ref in enumerate(out_refs):
                    take = slice(number * hidden, (number + 1) * hidden)
                    out_ref[value] = own_ref[0, :, take].astype(WIDE)
                    out_ref[1 - value] = other_ref[0, :, take].astype(WIDE)

    piece = pl.BlockSpec((1, rows, columns), lambda g: (g, 0, 0))
    outs = pl.pallas_call(
        kernel,
        grid=(fsdp,),
        in_specs=[pl.BlockSpec(memory_space=pltpu.SMEM), piece, piece],
        out_specs=[pl.BlockSpec((2, rows, hidden), lambda g: (0, 0, g))] * parts,
        out_shape=[jax.ShapeDtypeStruct((2, rows, fsdp * hidden), WIDE)] * parts,
    )(side, own, other)
    return [out.reshape(2 * rows, fsdp * hidden) for out in outs]


def widen_columns(side, own, other):
    fsdp, rows, columns = own.shape

    def kernel(side_ref, own_ref, other_ref, out_ref):
        for value in range(2):

            @pl.when(side_ref[0] == value)
            def _():
                out_ref[value * rows : (value + 1) * rows] = own_ref[0].astype(WIDE)
                out_ref[(1 - value) * rows : (2 - value) * rows] = other_ref[0].astype(WIDE)

    piece = pl.BlockSpec((1, rows, columns), lambda g: (g, 0, 0))
    return pl.pallas_call(
        kernel,
        grid=(fsdp,),
        in_specs=[pl.BlockSpec(memory_space=pltpu.SMEM), piece, piece],
        out_specs=pl.BlockSpec((2 * rows, columns), lambda g: (g, 0)),
        out_shape=jax.ShapeDtypeStruct((fsdp * 2 * rows, columns), WIDE),
    )(side, own, other)


def flip(value, axis, bit, size):
    return lax.ppermute(value, axis, [(place, place ^ bit) for place in range(size)])


def after(value, *earlier):
    return lax.optimization_barrier((value,) + earlier)[0]


def solution(mesh):
    fsdp = mesh.shape["fsdp"]
    ctx = mesh.shape["ctx"]
    tp = mesh.shape["tp"]

    def shift(value, step):
        return lax.ppermute(
            value, "fsdp", [(place, (place - step) % fsdp) for place in range(fsdp)]
        )

    def swap(value):
        return flip(value, "ctx", 1, ctx)

    def tp_gather(block):
        second = flip(block, "tp", 2, tp)
        pair = jnp.concatenate([block, second], axis=0)
        return jnp.concatenate([pair, flip(pair, "tp", 1, tp)], axis=0)

    def tp_scatter(make, rows):
        half = rows[0].shape[0] // 2
        sent = make(*(part[half:] for part in rows)).astype(LOW)
        got = flip(sent, "tp", 1, tp)
        kept = make(*(part[:half] for part in rows)) + got.astype(WIDE)
        sent_again = kept[half // 2 :].astype(LOW)
        return kept[: half // 2], flip(sent_again, "tp", 2, tp), sent, sent_again

    def local(
        inputs,
        out_grad,
        segments,
        w_query,
        w_key,
        w_value,
        w_out,
        w_gate,
        w_up,
        w_down,
        query_gain,
        key_gain,
        attn_gain,
        mlp_gain,
    ):
        f = lax.axis_index("fsdp")
        c = lax.axis_index("ctx")
        t = lax.axis_index("tp")
        half_len = inputs.shape[2]
        length = half_len * ctx
        part_len = length // tp
        block = D // fsdp
        half_block = block // 2
        heads_here = query_gain.shape[0]
        width = heads_here * HD
        hidden_here = w_gate.shape[1] // fsdp
        scale_factor = 1.0 / math.sqrt(HD)
        first = c == 0

        def pair(own, other, axis):
            return jnp.where(
                first,
                jnp.concatenate([own, other], axis=axis),
                jnp.concatenate([other, own], axis=axis),
            )

        def near_rows(value):
            return jnp.concatenate(
                [
                    lax.dynamic_slice_in_dim(value, (t ^ bit) * part_len, part_len, 0)
                    for bit in (0, 2, 1, 3)
                ],
                axis=0,
            )

        def plain_rows(value, size):
            parts = []
            for place in range(tp):
                far = t ^ place
                spot = (far & 1) * 2 + (far >> 1)
                parts.append(lax.dynamic_slice_in_dim(value, spot * size, size, 0))
            return jnp.concatenate(parts, axis=0)

        def place(r):
            return lax.rem(f + (r % fsdp), fsdp)

        gain_pack = jnp.concatenate(
            [query_gain.reshape(-1), key_gain.reshape(-1), attn_gain, mlp_gain]
        )[None]
        gain_near = jnp.concatenate(
            [gain_pack] + [shift(gain_pack, r) for r in range(1, fsdp)], axis=0
        )

        def half_of(shard, side):
            return lax.dynamic_slice_in_dim(shard, side * half_block, half_block, 0)

        def ring(own, earlier):
            moved = [half_of(own, c)]
            for r in range(1, fsdp):
                moved.append(shift(moved[-1] if r == 1 else after(moved[-1], *earlier), 1))
            whole = lax.dynamic_update_slice(
                jnp.zeros((D, own.shape[1]), LOW), after(own, moved[1]), (f * block, 0)
            )
            for r in range(1, fsdp):
                begin = place(r) * block
                whole = lax.dynamic_update_slice(whole, moved[r], (begin + c * half_block, 0))
                whole = lax.dynamic_update_slice(
                    whole, swap(moved[r]), (begin + (1 - c) * half_block, 0)
                )
            return with_layout_constraint(whole, Layout(major_to_minor=(0, 1))), moved

        qk_full, qk_moved = ring(jnp.concatenate([w_query, w_key], axis=1), (gain_near,))
        vo_full, vo_moved = ring(jnp.concatenate([w_value, w_out.T], axis=1), ())
        value_full, out_full = vo_full[:, :width], vo_full[:, width:]

        gain_all = lax.dynamic_slice_in_dim(
            jnp.concatenate([gain_near, gain_near], axis=0).astype(WIDE), lax.rem(fsdp - f, fsdp), fsdp, 0
        )
        qk_size = query_gain.size
        query_gain_row = (
            gain_all[:, :qk_size].reshape(fsdp, heads_here, -1).transpose(1, 0, 2).reshape(-1)
        )
        key_gain_row = (
            gain_all[:, qk_size : 2 * qk_size]
            .reshape(fsdp, heads_here, -1)
            .transpose(1, 0, 2)
            .reshape(-1)
        )
        attn_gains = gain_all[:, 2 * qk_size : 2 * qk_size + block].reshape(1, -1)
        mlp_gains = gain_all[:, 2 * qk_size + block : 2 * (qk_size + block)].reshape(1, -1)

        sub_len = half_len // tp
        tokens_kept = lax.dynamic_index_in_dim(inputs[:, 0], c, 0, keepdims=False)
        tokens_sent = lax.dynamic_slice(
            after(inputs, qk_moved[1]), (1 - c, 0, t * sub_len, 0), (1, 1, sub_len, D)
        )[0, 0]
        tokens_got = plain_rows(tp_gather(swap(tokens_sent)), sub_len)
        tokens = pair(tokens_kept, tokens_got, 0)
        segment_row = lax.dynamic_index_in_dim(segments[:, 0], c, 0, keepdims=False)

        half_hidden = hidden_here // 2

        def exchange(value):
            return lax.all_to_all(value, "fsdp", 0, 0, tiled=True)

        side = c[None]
        gate_sent, up_sent, down_sent = pack_sends(
            side, after(w_gate, qk_moved[1]), w_up, w_down, fsdp
        )
        gate_mine = exchange(after(gate_sent, qk_moved[-1]))
        up_mine = exchange(after(up_sent, gate_mine))
        down_mine = exchange(after(down_sent, up_mine))

        allowed = attention_mask(segment_row)
        cosine, sine_table = rotary_tables(doc_positions(segment_row))
        raw = product(tokens, qk_full)
        query_raw = raw[:, :width]
        key_raw = raw[:, width:]
        value_heads = product(tokens, value_full).astype(LOW).reshape(length, heads_here, HD)
        squares = lax.psum(
            jnp.stack([jnp.sum(query_raw * query_raw, axis=1), jnp.sum(key_raw * key_raw, axis=1)]),
            "tp",
        )
        squares, gate_mine = lax.optimization_barrier((squares, gate_mine))
        gate_other = swap(gate_mine)
        query_scale = lax.rsqrt(squares[0] / D + EPSILON)[:, None]
        key_scale = lax.rsqrt(squares[1] / D + EPSILON)[:, None]
        query_heads = rotate(
            (query_raw * query_scale * query_gain_row).reshape(length, heads_here, HD),
            cosine,
            sine_table,
        ).astype(LOW)
        key_heads = rotate(
            (key_raw * key_scale * key_gain_row).reshape(length, heads_here, HD),
            cosine,
            sine_table,
        ).astype(LOW)
        scores = head_scores(query_heads, key_heads, allowed)
        top_score = jnp.max(scores, axis=-1, keepdims=True)
        log_total = top_score + jnp.log(
            jnp.sum(jnp.exp(scores - top_score), axis=-1, keepdims=True)
        )
        probs_low = jnp.exp(scores - log_total).astype(LOW)
        probs_low, up_mine, gate_other = lax.optimization_barrier((probs_low, up_mine, gate_other))
        attended = (
            jnp.einsum("hqk,khd->qhd", probs_low, value_heads, preferred_element_type=WIDE)
            .astype(LOW)
            .reshape(length, width)
        )
        up_other = swap(up_mine)
        down_other = swap(down_mine)
        wide_full = place_wide(side, gate_mine, gate_other, up_mine, up_other)
        down_full = place_down(side, down_mine, down_other)
        attended_near = near_rows(attended)
        kept, again = tp_scatter(lambda rows: product_back(rows, out_full), (attended_near,))[:2]
        branch = kept + again.astype(WIDE)

        tokens_part = lax.dynamic_slice_in_dim(tokens, t * part_len, part_len, 0).astype(WIDE)
        branch_scale = lax.rsqrt(jnp.mean(branch * branch, axis=-1, keepdims=True) + EPSILON)
        hidden = tokens_part + branch * branch_scale * attn_gains
        hidden_low = hidden.astype(LOW)

        group_size = min(fsdp, 4)

        def to_owner(parts, gates=None):
            got = []
            for r in range(fsdp):
                kept, again = parts[r]
                if gates is not None and gates[r] is not None:
                    again = after(again, gates[r])
                part = kept + again.astype(WIDE)
                got.append(shift(part.astype(LOW), -r).astype(WIDE) if r else part)
            return sum(got[1:], got[0])

        def in_chunks(part, work):
            moved = [part]
            for _ in range(1, fsdp):
                moved.append(shift(moved[-1], 1))
            groups = []
            earlier = None
            for g in range(0, fsdp, group_size):
                group = jnp.zeros((group_size * length, D), LOW)
                for r in range(group_size):
                    second = flip(moved[g + r], "tp", 2, tp)
                    both = jnp.concatenate([moved[g + r], second], axis=0)
                    third = flip(both, "tp", 1, tp)
                    if earlier is not None:
                        third = after(third, earlier)
                    group = lax.dynamic_update_slice(group, both, (r * length, 0))
                    group = lax.dynamic_update_slice(
                        group, third, (r * length + length // 2, 0)
                    )
                    earlier = work(group[r * length : (r + 1) * length], g + r)
                groups.append(group)
            return groups

        wide_chunks, active_chunks, down_parts = [], [], []

        def forward(chunk, number):
            wide = product(chunk, wide_full)
            gate_value, up_value = wide[:, :hidden_here], wide[:, hidden_here:]
            active = (gate_value * jax.nn.sigmoid(gate_value) * up_value).astype(LOW)
            kept, again, sent, _ = tp_scatter(lambda rows: product(rows, down_full), (active,))
            down_parts.append((kept, again))
            wide_chunks.append(wide)
            active_chunks.append(active)
            return sent

        hidden_all = in_chunks(hidden_low, forward)
        down = to_owner(down_parts)

        down_scale = lax.rsqrt(jnp.mean(down * down, axis=-1, keepdims=True) + EPSILON)
        output_part = (hidden + down * down_scale * mlp_gains).astype(LOW)

        inner = lax.rem(t, tp // 2) * part_len
        grad_kept = lax.dynamic_slice(
            out_grad, (c, 0, inner, 0), (1, 1, part_len, D)
        )[0, 0]
        grad_sent = lax.dynamic_slice(
            out_grad, (1 - c, 0, inner, 0), (1, 1, part_len, D)
        )[0, 0]
        mine_here = t // (tp // 2) == c
        cotangent = jnp.where(
            mine_here, grad_kept, swap(after(grad_sent, qk_moved[-1]))
        ).astype(WIDE)

        scaled = cotangent * mlp_gains
        down_mean = jnp.mean(scaled * down, axis=-1, keepdims=True)
        down_low = (down_scale * (scaled - down * (down_scale * down_scale * down_mean))).astype(
            LOW
        )
        mlp_gain_grad = jnp.sum(cotangent * down * down_scale, axis=0)

        wide_lows, hidden_parts, last_sent = [], [], []

        def backward(chunk, number):
            wide = wide_chunks[number]
            gate_value, up_value = wide[:, :hidden_here], wide[:, hidden_here:]
            act_grad = product_back(chunk, down_full)
            sig = jax.nn.sigmoid(gate_value)
            gate_low = (act_grad * up_value * sig * (1.0 + gate_value * (1.0 - sig))).astype(LOW)
            up_low = (act_grad * gate_value * sig).astype(LOW)
            wide_low = jnp.concatenate([gate_low, up_low], axis=1)
            kept, again, sent, sent_again = tp_scatter(
                lambda rows: product_back(rows, wide_full), (wide_low,)
            )
            hidden_parts.append((kept, again))
            last_sent.append(sent_again)
            wide_lows.append(wide_low)
            return sent

        grad_all = in_chunks(down_low, backward)

        def spread(part):
            pairs = []
            for low_place in range(tp // 2):
                here, there = tp // 2 + low_place, tp + low_place
                pairs += [(here, there), (there, here)]
            got = lax.ppermute(part, ("ctx", "tp"), pairs)
            near = jnp.where(mine_here, part, got)
            far = flip(near, "tp", 2, tp)
            mine = jnp.where(mine_here, near, far)
            other = jnp.where(mine_here, far, near)
            both = jnp.where(
                first, jnp.stack([mine, other], 1), jnp.stack([other, mine], 1)
            )
            beside = flip(both, "tp", 1, tp)
            return jnp.where(
                t % 2 == 0,
                jnp.concatenate([both, beside], axis=2),
                jnp.concatenate([beside, both], axis=2),
            )

        def halves(split):
            return (
                lax.dynamic_index_in_dim(split, c, 1, keepdims=False),
                lax.dynamic_index_in_dim(split, 1 - c, 1, keepdims=False),
            )

        def half_sum(kept, sent):
            return (kept.astype(WIDE) + swap(sent).astype(WIDE)).astype(LOW)

        late = lax.optimization_barrier((*grad_all, *hidden_all, *last_sent))
        late_grad = late[: len(grad_all)]
        late_hidden = late[len(grad_all) : len(grad_all) + len(hidden_all)]
        down_split = grad_blocks(active_chunks, late_grad, fsdp, False)
        down_sum = lax.psum_scatter(down_split, "ctx", scatter_dimension=0)
        late_hidden = list(lax.optimization_barrier((*late_hidden, down_split)))[:-1]
        wide_split = grad_blocks(late_hidden, wide_lows, fsdp, True)
        wide_sum = lax.psum_scatter(wide_split, "ctx", scatter_dimension=0)
        hidden_grad = cotangent + after(to_owner(hidden_parts), wide_split)

        lifted = hidden_grad * attn_gains
        branch_mean = jnp.mean(lifted * branch, axis=-1, keepdims=True)
        branch_low = (
            branch_scale * (lifted - branch * (branch_scale * branch_scale * branch_mean))
        ).astype(LOW)
        attn_gain_grad = jnp.sum(hidden_grad * branch * branch_scale, axis=0)
        branch_low, down_sum = lax.optimization_barrier((branch_low, down_sum))
        down_back = exchange(down_sum)
        branch_near = tp_gather(branch_low)
        heads_grad = plain_rows(
            product(branch_near, out_full).astype(LOW), part_len
        ).reshape(length, heads_here, HD)
        attn_probs = jnp.exp(head_scores(query_heads, key_heads, allowed) - log_total)
        value_grad = (
            jnp.einsum(
                "hqk,qhd->khd", attn_probs.astype(LOW), heads_grad, preferred_element_type=WIDE
            )
            .astype(LOW)
            .reshape(length, width)
        )
        value_part = product_left(tokens, value_grad).astype(LOW)
        out_part = product_left(attended_near, branch_near).astype(LOW)
        heads_grad, out_part, value_part = lax.optimization_barrier(
            (heads_grad, out_part, value_part)
        )
        probs_grad = jnp.einsum(
            "qhd,khd->hqk", heads_grad, value_heads, preferred_element_type=WIDE
        )
        score_grad = (
            attn_probs * (probs_grad - jnp.sum(attn_probs * probs_grad, axis=-1, keepdims=True))
        ).astype(LOW)
        score_grad, down_back, wide_sum = lax.optimization_barrier(
            (score_grad, down_back, wide_sum)
        )
        down_other = swap(down_back)
        wide_back = exchange(wide_sum)
        query_grad = (
            jnp.einsum("hqk,khd->qhd", score_grad, key_heads, preferred_element_type=WIDE)
            * scale_factor
        )
        key_grad = (
            jnp.einsum("hqk,qhd->khd", score_grad, query_heads, preferred_element_type=WIDE)
            * scale_factor
        )
        query_norm_grad = rotate(query_grad, cosine, -sine_table).reshape(length, width)
        key_norm_grad = rotate(key_grad, cosine, -sine_table).reshape(length, width)
        query_term = query_norm_grad * query_gain_row
        key_term = key_norm_grad * key_gain_row
        sums = jnp.concatenate(
            [
                jnp.sum(query_term * query_raw, axis=1),
                jnp.sum(key_term * key_raw, axis=1),
                attn_gain_grad,
                mlp_gain_grad,
            ]
        )
        sums = lax.psum(sums, "tp")
        dots = sums[: 2 * length].reshape(2, length)
        rows_grad = sums[2 * length :].reshape(2, D)
        query_cube = query_scale * query_scale * query_scale
        key_cube = key_scale * key_scale * key_scale
        query_raw_grad = (
            query_scale * query_term - query_raw * (query_cube * dots[0][:, None] / D)
        ).astype(LOW)
        key_raw_grad = (
            key_scale * key_term - key_raw * (key_cube * dots[1][:, None] / D)
        ).astype(LOW)
        query_gain_grad = jnp.sum(query_norm_grad * query_raw * query_scale, axis=0)
        key_gain_grad = jnp.sum(key_norm_grad * key_raw * key_scale, axis=0)
        qk_grad = jnp.concatenate([query_raw_grad, key_raw_grad], axis=1)

        def scattered(partial, dim):
            return lax.psum_scatter(partial, "fsdp", scatter_dimension=dim, tiled=True)

        out_mine, value_mine = scattered(out_part, 1), scattered(value_part, 0)
        gain_part = jnp.concatenate(
            [
                rows_grad.reshape(2, fsdp, block).transpose(1, 0, 2).reshape(fsdp, 2 * block),
                jnp.stack([query_gain_grad, key_gain_grad])
                .reshape(2 * heads_here, fsdp, HD // fsdp)
                .transpose(1, 0, 2)
                .reshape(fsdp, -1),
            ],
            axis=1,
        )
        gain_rows = -(-gain_part.shape[1] // (16 * width)) * 16
        gain_part = jnp.pad(gain_part, ((0, 0), (0, gain_rows * width - gain_part.shape[1])))
        gain_part = lax.optimization_barrier(
            gain_part.astype(LOW).reshape(fsdp, gain_rows, width)
        )

        def half_grads(grads, more):
            kept, sent = halves(grads.astype(LOW).reshape(fsdp, 2, half_block, width))
            if more is not None:
                kept = jnp.concatenate([kept, more], axis=1)
                sent = jnp.concatenate([sent, more], axis=1)
            return kept, sent

        def own_sum(summed):
            return jnp.sum(exchange(summed).astype(WIDE), axis=0)

        def row_shard(mine):
            mine = lax.optimization_barrier(mine.astype(LOW))
            return pair(mine, swap(mine), 0).astype(WIDE)

        query_kept, query_sent = half_grads(product_left(tokens, query_raw_grad), gain_part)
        key_kept, key_sent = half_grads(
            product_left(tokens, after(key_raw_grad, query_sent)), None
        )
        query_sum, out_mine, value_mine, wide_back = lax.optimization_barrier(
            (half_sum(query_kept, query_sent), out_mine, value_mine, wide_back)
        )
        wide_far = swap(wide_back)
        grad_out, grad_value = lax.psum((out_mine, value_mine), "ctx")
        grad_down = widen_columns(side, down_back, down_other)
        query_mine = own_sum(query_sum)
        key_sum, grad_down = lax.optimization_barrier(
            (half_sum(key_kept, key_sent), grad_down)
        )
        grad_gate, grad_up = widen_rows(side, wide_back, wide_far, 2)
        key_mine, grad_out, grad_value, grad_gate, grad_up = lax.optimization_barrier(
            (own_sum(key_sum), grad_out, grad_value, grad_gate, grad_up)
        )
        grad_query = row_shard(query_mine[:half_block])
        grad_key = row_shard(key_mine)
        own_gains = query_mine[half_block:].reshape(-1)
        qk_grad, value_grad = lax.optimization_barrier((qk_grad, value_grad, key_sent))[:2]
        grad_out, grad_value = grad_out.astype(WIDE), grad_value.astype(WIDE)

        kept, again = tp_scatter(
            lambda rows, more: product_back(rows, qk_full) + product_back(more, value_full),
            (near_rows(qk_grad), near_rows(value_grad)),
        )[:2]
        input_part = hidden_grad + (kept + again.astype(WIDE))

        both_parts = lax.optimization_barrier(jnp.stack([output_part, input_part.astype(LOW)]))
        both_parts = spread(both_parts)[:, :, None]
        layer_out, layer_in_grad = both_parts[0], both_parts[1].astype(WIDE)

        sum_heads = own_gains[2 * block : 2 * block + 2 * heads_here * (HD // fsdp)].reshape(2, heads_here, HD // fsdp)
        return (
            layer_out,
            layer_in_grad,
            grad_query,
            grad_key,
            grad_value,
            grad_out,
            grad_gate,
            grad_up,
            grad_down,
            sum_heads[0],
            sum_heads[1],
            own_gains[:block],
            own_gains[block : 2 * block],
        )

    rows = P("fsdp", "tp")
    columns = P("tp", "fsdp")
    whole_tokens = P(None, "fsdp", "ctx", None)
    return jax.shard_map(
        local,
        mesh=mesh,
        in_specs=(
            whole_tokens,
            whole_tokens,
            P(None, "fsdp", None),
            rows,
            rows,
            rows,
            columns,
            rows,
            rows,
            columns,
            columns,
            columns,
            P("fsdp"),
            P("fsdp"),
        ),
        out_specs=(
            whole_tokens,
            whole_tokens,
            rows,
            rows,
            rows,
            columns,
            rows,
            rows,
            columns,
            columns,
            columns,
            P("fsdp"),
            P("fsdp"),
        ),
        check_vma=False,
    )
```

```python
import math

import jax
import jax.numpy as jnp
from jax import lax
from jax.experimental import pallas as pl
from jax.experimental.layout import Layout, with_layout_constraint
from jax.experimental.pallas import tpu as pltpu
from jax.sharding import PartitionSpec as P

D = 2048
HD = 128
EPSILON = 1e-06
ROTARY_BASE = 500000.0
MASKED = -1e30
LOW = jnp.bfloat16
WIDE = jnp.float32


def product(left_side, right_side):
    return jnp.dot(left_side, right_side, preferred_element_type=WIDE)


def product_back(left_side, right_side):
    return lax.dot_general(
        left_side, right_side, (((1,), (1,)), ((), ())), preferred_element_type=WIDE
    )


def product_left(left_side, right_side):
    return lax.dot_general(
        left_side, right_side, (((0,), (0,)), ((), ())), preferred_element_type=WIDE
    )


def doc_positions(segment_row):
    earlier = (segment_row[None, :] < segment_row[:, None]).astype(jnp.int32)
    return jnp.arange(segment_row.shape[0], dtype=jnp.int32) - jnp.sum(earlier, axis=1)


def rotary_tables(positions):
    half_size = HD // 2
    frequency = ROTARY_BASE ** (-(jnp.arange(half_size, dtype=WIDE) * 2.0 / HD))
    angle_table = positions.astype(WIDE)[:, None] * frequency[None, :]
    return (jnp.cos(angle_table)[:, None, :], jnp.sin(angle_table)[:, None, :])


def rotate(values, cosine, sine_table):
    half_size = values.shape[-1] // 2
    first_half = values[..., :half_size]
    second_half = values[..., half_size:]
    return jnp.concatenate(
        [
            first_half * cosine - second_half * sine_table,
            second_half * cosine + first_half * sine_table,
        ],
        axis=-1,
    )


def attention_mask(segment_row):
    places = jnp.arange(segment_row.shape[0])
    return (segment_row[:, None] == segment_row[None, :]) & (places[None, :] <= places[:, None])


def head_scores(query_heads, key_heads, allowed):
    raw_scores = jnp.einsum(
        "qhd,khd->hqk", query_heads, key_heads, preferred_element_type=WIDE
    ) * (1.0 / math.sqrt(HD))
    return jnp.where(allowed[None], raw_scores, MASKED)


def grad_blocks(lefts, rights, fsdp, split_left):
    rows, columns = lefts[0].shape[1], rights[0].shape[1]
    if split_left:
        rows = rows // fsdp
    else:
        columns = columns // fsdp
    half = rows // 2

    def kernel(*refs):
        left_refs, right_refs = refs[: len(lefts)], refs[len(lefts) : -1]
        out_ref = refs[-1]
        pieces = max(len(lefts), len(rights))

        def part(group, number):
            per = pieces // len(group)
            ref = group[number // per]
            size = ref.shape[0] // per
            start = (number % per) * size
            return ref[start : start + size, :]

        total = 0.0
        for number in range(pieces):
            total = total + lax.dot_general(
                part(left_refs, number),
                part(right_refs, number),
                (((0,), (0,)), ((), ())),
                preferred_element_type=WIDE,
            )
        out_ref[0, 0] = total[:half].astype(LOW)
        out_ref[1, 0] = total[half:].astype(LOW)

    def moving(size, width):
        return pl.BlockSpec((size, width), lambda g: (0, g))

    def fixed(size, width):
        return pl.BlockSpec((size, width), lambda g: (0, 0))

    left_spec, right_spec = (moving, fixed) if split_left else (fixed, moving)
    return pl.pallas_call(
        kernel,
        grid=(fsdp,),
        in_specs=[left_spec(left.shape[0], rows) for left in lefts]
        + [right_spec(right.shape[0], columns) for right in rights],
        out_specs=pl.BlockSpec((2, 1, half, columns), lambda g: (0, g, 0, 0)),
        out_shape=jax.ShapeDtypeStruct((2, fsdp, half, columns), LOW),
        compiler_params=pltpu.CompilerParams(vmem_limit_bytes=50 * 1024 * 1024),
        cost_estimate=pl.CostEstimate(flops=1, bytes_accessed=1, transcendentals=0),
    )(*lefts, *rights)


def pack_sends(side, w_gate, w_up, w_down, fsdp):
    rows, hidden = w_gate.shape[0] // 2, w_gate.shape[1] // fsdp
    down_rows, columns = hidden // 2, w_down.shape[1]

    def kernel(side_ref, gate_ref, up_ref, down_ref, gate_out, up_out, down_out):
        gate_out[0] = gate_ref[...]
        up_out[0] = up_ref[...]
        down_out[0] = down_ref[...]

    wide_in = pl.BlockSpec((rows, hidden), lambda g, chosen: (chosen[0], g))
    wide_out = pl.BlockSpec((1, rows, hidden), lambda g, chosen: (g, 0, 0))
    return pl.pallas_call(
        kernel,
        grid_spec=pltpu.PrefetchScalarGridSpec(
            num_scalar_prefetch=1,
            grid=(fsdp,),
            in_specs=[
                wide_in,
                wide_in,
                pl.BlockSpec((down_rows, columns), lambda g, chosen: (2 * g + chosen[0], 0)),
            ],
            out_specs=[
                wide_out,
                wide_out,
                pl.BlockSpec((1, down_rows, columns), lambda g, chosen: (g, 0, 0)),
            ],
        ),
        out_shape=[
            jax.ShapeDtypeStruct((fsdp, rows, hidden), w_gate.dtype),
            jax.ShapeDtypeStruct((fsdp, rows, hidden), w_gate.dtype),
            jax.ShapeDtypeStruct((fsdp, down_rows, columns), w_gate.dtype),
        ],
    )(side, w_gate, w_up, w_down)


def place_wide(side, gate_own, gate_other, up_own, up_other):
    fsdp, rows, hidden = gate_own.shape

    def kernel(side_ref, gate_a, gate_b, up_a, up_b, out_ref):
        for value in range(2):

            @pl.when(side_ref[0] == value)
            def _():
                mine = slice(value * rows, (value + 1) * rows)
                others = slice((1 - value) * rows, (2 - value) * rows)
                out_ref[mine, :hidden] = gate_a[0]
                out_ref[others, :hidden] = gate_b[0]
                out_ref[mine, hidden:] = up_a[0]
                out_ref[others, hidden:] = up_b[0]

    piece = pl.BlockSpec((1, rows, hidden), lambda g: (g, 0, 0))
    return pl.pallas_call(
        kernel,
        grid=(fsdp,),
        in_specs=[pl.BlockSpec(memory_space=pltpu.SMEM)] + [piece] * 4,
        out_specs=pl.BlockSpec((2 * rows, 2 * hidden), lambda g: (g, 0)),
        out_shape=jax.ShapeDtypeStruct((fsdp * 2 * rows, 2 * hidden), gate_own.dtype),
    )(side, gate_own, gate_other, up_own, up_other)


def place_down(side, own, other):
    fsdp, rows, columns = own.shape

    def kernel(side_ref, own_ref, other_ref, out_ref):
        for value in range(2):

            @pl.when(side_ref[0] == value)
            def _():
                out_ref[value * rows : (value + 1) * rows, :] = own_ref[0]
                out_ref[(1 - value) * rows : (2 - value) * rows, :] = other_ref[0]

    piece = pl.BlockSpec((1, rows, columns), lambda g: (g, 0, 0))
    return pl.pallas_call(
        kernel,
        grid=(fsdp,),
        in_specs=[pl.BlockSpec(memory_space=pltpu.SMEM), piece, piece],
        out_specs=pl.BlockSpec((2 * rows, columns), lambda g: (0, g)),
        out_shape=jax.ShapeDtypeStruct((2 * rows, fsdp * columns), own.dtype),
    )(side, own, other)


def widen_rows(side, own, other, parts):
    fsdp, rows, columns = own.shape
    hidden = columns // parts

    def kernel(side_ref, own_ref, other_ref, *out_refs):
        for value in range(2):

            @pl.when(side_ref[0] == value)
            def _():
                for number, out_ref in enumerate(out_refs):
                    take = slice(number * hidden, (number + 1) * hidden)
                    out_ref[value] = own_ref[0, :, take].astype(WIDE)
                    out_ref[1 - value] = other_ref[0, :, take].astype(WIDE)

    piece = pl.BlockSpec((1, rows, columns), lambda g: (g, 0, 0))
    outs = pl.pallas_call(
        kernel,
        grid=(fsdp,),
        in_specs=[pl.BlockSpec(memory_space=pltpu.SMEM), piece, piece],
        out_specs=[pl.BlockSpec((2, rows, hidden), lambda g: (0, 0, g))] * parts,
        out_shape=[jax.ShapeDtypeStruct((2, rows, fsdp * hidden), WIDE)] * parts,
    )(side, own, other)
    return [out.reshape(2 * rows, fsdp * hidden) for out in outs]


def widen_columns(side, own, other):
    fsdp, rows, columns = own.shape

    def kernel(side_ref, own_ref, other_ref, out_ref):
        for value in range(2):

            @pl.when(side_ref[0] == value)
            def _():
                out_ref[value * rows : (value + 1) * rows] = own_ref[0].astype(WIDE)
                out_ref[(1 - value) * rows : (2 - value) * rows] = other_ref[0].astype(WIDE)

    piece = pl.BlockSpec((1, rows, columns), lambda g: (g, 0, 0))
    return pl.pallas_call(
        kernel,
        grid=(fsdp,),
        in_specs=[pl.BlockSpec(memory_space=pltpu.SMEM), piece, piece],
        out_specs=pl.BlockSpec((2 * rows, columns), lambda g: (g, 0)),
        out_shape=jax.ShapeDtypeStruct((fsdp * 2 * rows, columns), WIDE),
    )(side, own, other)


def flip(value, axis, bit, size):
    return lax.ppermute(value, axis, [(place, place ^ bit) for place in range(size)])


def after(value, *earlier):
    return lax.optimization_barrier((value,) + earlier)[0]


def solution(mesh):
    fsdp = mesh.shape["fsdp"]
    ctx = mesh.shape["ctx"]
    tp = mesh.shape["tp"]

    def shift(value, step):
        return lax.ppermute(
            value, "fsdp", [(place, (place - step) % fsdp) for place in range(fsdp)]
        )

    def swap(value):
        return flip(value, "ctx", 1, ctx)

    def tp_gather(block):
        second = flip(block, "tp", 2, tp)
        pair = jnp.concatenate([block, second], axis=0)
        return jnp.concatenate([pair, flip(pair, "tp", 1, tp)], axis=0)

    def tp_scatter(make, rows):
        half = rows[0].shape[0] // 2
        sent = make(*(part[half:] for part in rows)).astype(LOW)
        got = flip(sent, "tp", 1, tp)
        kept = make(*(part[:half] for part in rows)) + got.astype(WIDE)
        sent_again = kept[half // 2 :].astype(LOW)
        return kept[: half // 2], flip(sent_again, "tp", 2, tp), sent, sent_again

    def local(
        inputs,
        out_grad,
        segments,
        w_query,
        w_key,
        w_value,
        w_out,
        w_gate,
        w_up,
        w_down,
        query_gain,
        key_gain,
        attn_gain,
        mlp_gain,
    ):
        f = lax.axis_index("fsdp")
        c = lax.axis_index("ctx")
        t = lax.axis_index("tp")
        half_len = inputs.shape[2]
        length = half_len * ctx
        part_len = length // tp
        block = D // fsdp
        half_block = block // 2
        heads_here = query_gain.shape[0]
        width = heads_here * HD
        hidden_here = w_gate.shape[1] // fsdp
        scale_factor = 1.0 / math.sqrt(HD)
        first = c == 0

        def pair(own, other, axis):
            return jnp.where(
                first,
                jnp.concatenate([own, other], axis=axis),
                jnp.concatenate([other, own], axis=axis),
            )

        def near_rows(value):
            return jnp.concatenate(
                [
                    lax.dynamic_slice_in_dim(value, (t ^ bit) * part_len, part_len, 0)
                    for bit in (0, 2, 1, 3)
                ],
                axis=0,
            )

        def plain_rows(value, size):
            parts = []
            for place in range(tp):
                far = t ^ place
                spot = (far & 1) * 2 + (far >> 1)
                parts.append(lax.dynamic_slice_in_dim(value, spot * size, size, 0))
            return jnp.concatenate(parts, axis=0)

        def place(r):
            return lax.rem(f + (r % fsdp), fsdp)

        gain_pack = jnp.concatenate(
            [query_gain.reshape(-1), key_gain.reshape(-1), attn_gain, mlp_gain]
        )[None]
        gain_near = jnp.concatenate(
            [gain_pack] + [shift(gain_pack, r) for r in range(1, fsdp)], axis=0
        )

        def half_of(shard, side):
            return lax.dynamic_slice_in_dim(shard, side * half_block, half_block, 0)

        def ring(own, earlier):
            moved = [half_of(own, c)]
            for r in range(1, fsdp):
                moved.append(shift(moved[-1] if r == 1 else after(moved[-1], *earlier), 1))
            whole = lax.dynamic_update_slice(
                jnp.zeros((D, own.shape[1]), LOW), after(own, moved[1]), (f * block, 0)
            )
            for r in range(1, fsdp):
                begin = place(r) * block
                whole = lax.dynamic_update_slice(whole, moved[r], (begin + c * half_block, 0))
                whole = lax.dynamic_update_slice(
                    whole, swap(moved[r]), (begin + (1 - c) * half_block, 0)
                )
            return with_layout_constraint(whole, Layout(major_to_minor=(0, 1))), moved

        qk_full, qk_moved = ring(jnp.concatenate([w_query, w_key], axis=1), (gain_near,))
        vo_full, vo_moved = ring(jnp.concatenate([w_value, w_out.T], axis=1), ())
        value_full, out_full = vo_full[:, :width], vo_full[:, width:]

        gain_all = lax.dynamic_slice_in_dim(
            jnp.concatenate([gain_near, gain_near], axis=0).astype(WIDE), lax.rem(fsdp - f, fsdp), fsdp, 0
        )
        qk_size = query_gain.size
        query_gain_row = (
            gain_all[:, :qk_size].reshape(fsdp, heads_here, -1).transpose(1, 0, 2).reshape(-1)
        )
        key_gain_row = (
            gain_all[:, qk_size : 2 * qk_size]
            .reshape(fsdp, heads_here, -1)
            .transpose(1, 0, 2)
            .reshape(-1)
        )
        attn_gains = gain_all[:, 2 * qk_size : 2 * qk_size + block].reshape(1, -1)
        mlp_gains = gain_all[:, 2 * qk_size + block : 2 * (qk_size + block)].reshape(1, -1)

        sub_len = half_len // tp
        tokens_kept = lax.dynamic_index_in_dim(inputs[:, 0], c, 0, keepdims=False)
        tokens_sent = lax.dynamic_slice(
            after(inputs, qk_moved[1]), (1 - c, 0, t * sub_len, 0), (1, 1, sub_len, D)
        )[0, 0]
        tokens_got = plain_rows(tp_gather(swap(tokens_sent)), sub_len)
        tokens = pair(tokens_kept, tokens_got, 0)
        segment_row = lax.dynamic_index_in_dim(segments[:, 0], c, 0, keepdims=False)

        half_hidden = hidden_here // 2

        def exchange(value):
            return lax.all_to_all(value, "fsdp", 0, 0, tiled=True)

        side = c[None]
        gate_sent, up_sent, down_sent = pack_sends(
            side, after(w_gate, qk_moved[1]), w_up, w_down, fsdp
        )
        gate_mine = exchange(after(gate_sent, qk_moved[-1]))
        up_mine = exchange(after(up_sent, gate_mine))
        down_mine = exchange(after(down_sent, up_mine))

        allowed = attention_mask(segment_row)
        cosine, sine_table = rotary_tables(doc_positions(segment_row))
        raw = product(tokens, qk_full)
        query_raw = raw[:, :width]
        key_raw = raw[:, width:]
        value_heads = product(tokens, value_full).astype(LOW).reshape(length, heads_here, HD)
        squares = lax.psum(
            jnp.stack([jnp.sum(query_raw * query_raw, axis=1), jnp.sum(key_raw * key_raw, axis=1)]),
            "tp",
        )
        squares, gate_mine = lax.optimization_barrier((squares, gate_mine))
        gate_other = swap(gate_mine)
        query_scale = lax.rsqrt(squares[0] / D + EPSILON)[:, None]
        key_scale = lax.rsqrt(squares[1] / D + EPSILON)[:, None]
        query_heads = rotate(
            (query_raw * query_scale * query_gain_row).reshape(length, heads_here, HD),
            cosine,
            sine_table,
        ).astype(LOW)
        key_heads = rotate(
            (key_raw * key_scale * key_gain_row).reshape(length, heads_here, HD),
            cosine,
            sine_table,
        ).astype(LOW)
        scores = head_scores(query_heads, key_heads, allowed)
        top_score = jnp.max(scores, axis=-1, keepdims=True)
        log_total = top_score + jnp.log(
            jnp.sum(jnp.exp(scores - top_score), axis=-1, keepdims=True)
        )
        probs_low = jnp.exp(scores - log_total).astype(LOW)
        probs_low, up_mine, gate_other = lax.optimization_barrier((probs_low, up_mine, gate_other))
        attended = (
            jnp.einsum("hqk,khd->qhd", probs_low, value_heads, preferred_element_type=WIDE)
            .astype(LOW)
            .reshape(length, width)
        )
        up_other = swap(up_mine)
        down_other = swap(down_mine)
        wide_full = place_wide(side, gate_mine, gate_other, up_mine, up_other)
        down_full = place_down(side, down_mine, down_other)
        attended_near = near_rows(attended)
        kept, again = tp_scatter(lambda rows: product_back(rows, out_full), (attended_near,))[:2]
        branch = kept + again.astype(WIDE)

        tokens_part = lax.dynamic_slice_in_dim(tokens, t * part_len, part_len, 0).astype(WIDE)
        branch_scale = lax.rsqrt(jnp.mean(branch * branch, axis=-1, keepdims=True) + EPSILON)
        hidden = tokens_part + branch * branch_scale * attn_gains
        hidden_low = hidden.astype(LOW)

        group_size = min(fsdp, 4)

        def to_owner(parts, gates=None):
            got = []
            for r in range(fsdp):
                kept, again = parts[r]
                if gates is not None and gates[r] is not None:
                    again = after(again, gates[r])
                part = kept + again.astype(WIDE)
                got.append(shift(part.astype(LOW), -r).astype(WIDE) if r else part)
            return sum(got[1:], got[0])

        def in_chunks(part, work):
            moved = [part]
            for _ in range(1, fsdp):
                moved.append(shift(moved[-1], 1))
            groups = []
            done = []
            for g in range(0, fsdp, group_size):
                group = jnp.zeros((group_size * length, D), LOW)
                for r in range(group_size):
                    second = flip(moved[g + r], "tp", 2, tp)
                    both = jnp.concatenate([moved[g + r], second], axis=0)
                    third = flip(both, "tp", 1, tp)
                    if done:
                        third = after(third, done[-1][0])
                    if len(done) > 1:
                        third = after(third, done[-2][1])
                    group = lax.dynamic_update_slice(group, both, (r * length, 0))
                    group = lax.dynamic_update_slice(
                        group, third, (r * length + length // 2, 0)
                    )
                    done.append(work(group[r * length : (r + 1) * length], g + r))
                groups.append(group)
            return groups

        wide_chunks, active_chunks, down_parts = [], [], []

        def forward(chunk, number):
            wide = product(chunk, wide_full)
            gate_value, up_value = wide[:, :hidden_here], wide[:, hidden_here:]
            active = (gate_value * jax.nn.sigmoid(gate_value) * up_value).astype(LOW)
            kept, again, sent, _ = tp_scatter(lambda rows: product(rows, down_full), (active,))
            down_parts.append((kept, again))
            wide_chunks.append(wide)
            active_chunks.append(active)
            return sent, again

        hidden_all = in_chunks(hidden_low, forward)
        down = to_owner(down_parts)

        down_scale = lax.rsqrt(jnp.mean(down * down, axis=-1, keepdims=True) + EPSILON)
        output_part = (hidden + down * down_scale * mlp_gains).astype(LOW)

        inner = lax.rem(t, tp // 2) * part_len
        grad_kept = lax.dynamic_slice(
            out_grad, (c, 0, inner, 0), (1, 1, part_len, D)
        )[0, 0]
        grad_sent = lax.dynamic_slice(
            out_grad, (1 - c, 0, inner, 0), (1, 1, part_len, D)
        )[0, 0]
        mine_here = t // (tp // 2) == c
        cotangent = jnp.where(
            mine_here, grad_kept, swap(after(grad_sent, qk_moved[-1]))
        ).astype(WIDE)

        scaled = cotangent * mlp_gains
        down_mean = jnp.mean(scaled * down, axis=-1, keepdims=True)
        down_low = (down_scale * (scaled - down * (down_scale * down_scale * down_mean))).astype(
            LOW
        )
        mlp_gain_grad = jnp.sum(cotangent * down * down_scale, axis=0)

        wide_lows, hidden_parts, last_sent = [], [], []

        def backward(chunk, number):
            wide = wide_chunks[number]
            gate_value, up_value = wide[:, :hidden_here], wide[:, hidden_here:]
            act_grad = product_back(chunk, down_full)
            sig = jax.nn.sigmoid(gate_value)
            gate_low = (act_grad * up_value * sig * (1.0 + gate_value * (1.0 - sig))).astype(LOW)
            up_low = (act_grad * gate_value * sig).astype(LOW)
            wide_low = jnp.concatenate([gate_low, up_low], axis=1)
            kept, again, sent, sent_again = tp_scatter(
                lambda rows: product_back(rows, wide_full), (wide_low,)
            )
            hidden_parts.append((kept, again))
            last_sent.append(sent_again)
            wide_lows.append(wide_low)
            return sent, again

        grad_all = in_chunks(down_low, backward)

        def spread(part):
            pairs = []
            for low_place in range(tp // 2):
                here, there = tp // 2 + low_place, tp + low_place
                pairs += [(here, there), (there, here)]
            got = lax.ppermute(part, ("ctx", "tp"), pairs)
            near = jnp.where(mine_here, part, got)
            far = flip(near, "tp", 2, tp)
            mine = jnp.where(mine_here, near, far)
            other = jnp.where(mine_here, far, near)
            both = jnp.where(
                first, jnp.stack([mine, other], 1), jnp.stack([other, mine], 1)
            )
            beside = flip(both, "tp", 1, tp)
            return jnp.where(
                t % 2 == 0,
                jnp.concatenate([both, beside], axis=2),
                jnp.concatenate([beside, both], axis=2),
            )

        def halves(split):
            return (
                lax.dynamic_index_in_dim(split, c, 1, keepdims=False),
                lax.dynamic_index_in_dim(split, 1 - c, 1, keepdims=False),
            )

        def half_sum(kept, sent):
            return (kept.astype(WIDE) + swap(sent).astype(WIDE)).astype(LOW)

        late = lax.optimization_barrier((*grad_all, *hidden_all, *last_sent))
        late_grad = late[: len(grad_all)]
        late_hidden = late[len(grad_all) : len(grad_all) + len(hidden_all)]
        down_split = grad_blocks(active_chunks, late_grad, fsdp, False)
        down_sum = lax.psum_scatter(down_split, "ctx", scatter_dimension=0)
        late_hidden = list(lax.optimization_barrier((*late_hidden, down_split)))[:-1]
        wide_split = grad_blocks(late_hidden, wide_lows, fsdp, True)
        wide_sum = lax.psum_scatter(wide_split, "ctx", scatter_dimension=0)
        hidden_grad = cotangent + after(to_owner(hidden_parts), wide_split)

        lifted = hidden_grad * attn_gains
        branch_mean = jnp.mean(lifted * branch, axis=-1, keepdims=True)
        branch_low = (
            branch_scale * (lifted - branch * (branch_scale * branch_scale * branch_mean))
        ).astype(LOW)
        attn_gain_grad = jnp.sum(hidden_grad * branch * branch_scale, axis=0)
        branch_low, down_sum = lax.optimization_barrier((branch_low, down_sum))
        down_back = exchange(down_sum)
        branch_near = tp_gather(branch_low)
        heads_grad = plain_rows(
            product(branch_near, out_full).astype(LOW), part_len
        ).reshape(length, heads_here, HD)
        attn_probs = jnp.exp(head_scores(query_heads, key_heads, allowed) - log_total)
        value_grad = (
            jnp.einsum(
                "hqk,qhd->khd", attn_probs.astype(LOW), heads_grad, preferred_element_type=WIDE
            )
            .astype(LOW)
            .reshape(length, width)
        )
        value_part = product_left(tokens, value_grad).astype(LOW)
        out_part = product_left(attended_near, branch_near).astype(LOW)
        heads_grad, out_part, value_part = lax.optimization_barrier(
            (heads_grad, out_part, value_part)
        )
        probs_grad = jnp.einsum(
            "qhd,khd->hqk", heads_grad, value_heads, preferred_element_type=WIDE
        )
        score_grad = (
            attn_probs * (probs_grad - jnp.sum(attn_probs * probs_grad, axis=-1, keepdims=True))
        ).astype(LOW)
        score_grad, down_back, wide_sum = lax.optimization_barrier(
            (score_grad, down_back, wide_sum)
        )
        down_other = swap(down_back)
        wide_back = exchange(wide_sum)
        query_grad = (
            jnp.einsum("hqk,khd->qhd", score_grad, key_heads, preferred_element_type=WIDE)
            * scale_factor
        )
        key_grad = (
            jnp.einsum("hqk,qhd->khd", score_grad, query_heads, preferred_element_type=WIDE)
            * scale_factor
        )
        query_norm_grad = rotate(query_grad, cosine, -sine_table).reshape(length, width)
        key_norm_grad = rotate(key_grad, cosine, -sine_table).reshape(length, width)
        query_term = query_norm_grad * query_gain_row
        key_term = key_norm_grad * key_gain_row
        sums = jnp.concatenate(
            [
                jnp.sum(query_term * query_raw, axis=1),
                jnp.sum(key_term * key_raw, axis=1),
                attn_gain_grad,
                mlp_gain_grad,
            ]
        )
        sums = lax.psum(sums, "tp")
        dots = sums[: 2 * length].reshape(2, length)
        rows_grad = sums[2 * length :].reshape(2, D)
        query_cube = query_scale * query_scale * query_scale
        key_cube = key_scale * key_scale * key_scale
        query_raw_grad = (
            query_scale * query_term - query_raw * (query_cube * dots[0][:, None] / D)
        ).astype(LOW)
        key_raw_grad = (
            key_scale * key_term - key_raw * (key_cube * dots[1][:, None] / D)
        ).astype(LOW)
        query_gain_grad = jnp.sum(query_norm_grad * query_raw * query_scale, axis=0)
        key_gain_grad = jnp.sum(key_norm_grad * key_raw * key_scale, axis=0)
        qk_grad = jnp.concatenate([query_raw_grad, key_raw_grad], axis=1)

        def scattered(partial, dim):
            return lax.psum_scatter(partial, "fsdp", scatter_dimension=dim, tiled=True)

        out_mine, value_mine = scattered(out_part, 1), scattered(value_part, 0)
        gain_part = jnp.concatenate(
            [
                rows_grad.reshape(2, fsdp, block).transpose(1, 0, 2).reshape(fsdp, 2 * block),
                jnp.stack([query_gain_grad, key_gain_grad])
                .reshape(2 * heads_here, fsdp, HD // fsdp)
                .transpose(1, 0, 2)
                .reshape(fsdp, -1),
            ],
            axis=1,
        )
        gain_rows = -(-gain_part.shape[1] // (16 * width)) * 16
        gain_part = jnp.pad(gain_part, ((0, 0), (0, gain_rows * width - gain_part.shape[1])))
        gain_part = lax.optimization_barrier(
            gain_part.astype(LOW).reshape(fsdp, gain_rows, width)
        )

        def half_grads(grads, more):
            kept, sent = halves(grads.astype(LOW).reshape(fsdp, 2, half_block, width))
            if more is not None:
                kept = jnp.concatenate([kept, more], axis=1)
                sent = jnp.concatenate([sent, more], axis=1)
            return kept, sent

        def own_sum(summed):
            return jnp.sum(exchange(summed).astype(WIDE), axis=0)

        def row_shard(mine):
            mine = lax.optimization_barrier(mine.astype(LOW))
            return pair(mine, swap(mine), 0).astype(WIDE)

        query_kept, query_sent = half_grads(product_left(tokens, query_raw_grad), gain_part)
        key_kept, key_sent = half_grads(
            product_left(tokens, after(key_raw_grad, query_sent)), None
        )
        query_sum, out_mine, value_mine, wide_back = lax.optimization_barrier(
            (half_sum(query_kept, query_sent), out_mine, value_mine, wide_back)
        )
        wide_far = swap(wide_back)
        grad_out, grad_value = lax.psum((out_mine, value_mine), "ctx")
        grad_down = widen_columns(side, down_back, down_other)
        query_mine = own_sum(query_sum)
        key_sum, grad_down = lax.optimization_barrier(
            (half_sum(key_kept, key_sent), grad_down)
        )
        grad_gate, grad_up = widen_rows(side, wide_back, wide_far, 2)
        key_mine, grad_out, grad_value, grad_gate, grad_up = lax.optimization_barrier(
            (own_sum(key_sum), grad_out, grad_value, grad_gate, grad_up)
        )
        grad_query = row_shard(query_mine[:half_block])
        grad_key = row_shard(key_mine)
        own_gains = query_mine[half_block:].reshape(-1)
        qk_grad, value_grad = lax.optimization_barrier((qk_grad, value_grad, key_sent))[:2]
        grad_out, grad_value = grad_out.astype(WIDE), grad_value.astype(WIDE)

        kept, again = tp_scatter(
            lambda rows, more: product_back(rows, qk_full) + product_back(more, value_full),
            (near_rows(qk_grad), near_rows(value_grad)),
        )[:2]
        input_part = hidden_grad + (kept + again.astype(WIDE))

        both_parts = lax.optimization_barrier(jnp.stack([output_part, input_part.astype(LOW)]))
        both_parts = spread(both_parts)[:, :, None]
        layer_out, layer_in_grad = both_parts[0], both_parts[1].astype(WIDE)

        sum_heads = own_gains[2 * block : 2 * block + 2 * heads_here * (HD // fsdp)].reshape(2, heads_here, HD // fsdp)
        return (
            layer_out,
            layer_in_grad,
            grad_query,
            grad_key,
            grad_value,
            grad_out,
            grad_gate,
            grad_up,
            grad_down,
            sum_heads[0],
            sum_heads[1],
            own_gains[:block],
            own_gains[block : 2 * block],
        )

    rows = P("fsdp", "tp")
    columns = P("tp", "fsdp")
    whole_tokens = P(None, "fsdp", "ctx", None)
    return jax.shard_map(
        local,
        mesh=mesh,
        in_specs=(
            whole_tokens,
            whole_tokens,
            P(None, "fsdp", None),
            rows,
            rows,
            rows,
            columns,
            rows,
            rows,
            columns,
            columns,
            columns,
            P("fsdp"),
            P("fsdp"),
        ),
        out_specs=(
            whole_tokens,
            whole_tokens,
            rows,
            rows,
            rows,
            columns,
            rows,
            rows,
            columns,
            columns,
            columns,
            P("fsdp"),
            P("fsdp"),
        ),
        check_vma=False,
    )
```
